128 devices in a mesh: grp: 8 (over x, core), tie: 16 (over y, z).
Axes of the slice: x: 4, y: 4, z: 4, core: 2. Of those that a mesh axis runs over, the one named last changes fastest.
Arguments:
- soil_disp: bfloat16 [64, 32768], P(None, ('grp', 'tie')), may hold values from -6 to 6
- soil_vals: bfloat16 [7, 64, 64, 32768], P(None, None, None, ('grp', 'tie')), may hold values from -0.25 to 0.25
- soil_cols: int32 [7, 32768], P(None, ('grp', 'tie')), may hold values from 0 to 319, as said below
- load: float32 [64, 32768], P(None, ('grp', 'tie')), may hold values from -6 to 6
- pile_disp: bfloat16 [64, 131072], P(None, ('grp', 'tie')), may hold values from -6 to 6
- tie_vals: bfloat16 [64, 64, 131072], P(None, None, ('grp', 'tie')), may hold values from -0.75 to 0.75
- tie_pile: int32 [131072], P(('grp', 'tie')), may hold values from 0 to 16383, as said below
- tie_limit: float32 [131072], P(('grp', 'tie')), may hold values from 0.3 to 3
- tie_dest: int32 [131072], P(('grp', 'tie')), may hold values from 0 to 127, as said below
- tie_block: int32 [131072], P(('grp', 'tie')), may hold values from 0 to 255
Outputs:
- residual: float32 [64, 32768], P(None, ('grp', 'tie'))
The draws below stay inside these ranges and needn't reach their ends.
Inputs may be any that keep to these rules, and one draw needn't show every extreme that they name: soil_cols[0, s] is 32 plus the block's own position on its device; the others lie within 32 blocks of it. On each device ties are listed by nondecreasing tie_dest; one device names one destination at most 16 times, and some destination is named exactly 16 times by every device. `tie_pile`: group segment q is held by the group's device q // 1024; the ties of one device name segments of one such device at most 128 times, and every device names some such device exactly 128 times.
All inputs are finite; a program needn't handle non-finite values.
Results may differ from the reference program's by a relative error of at most 0.0045.
Values may be sent and summed in bfloat16 or wider, within the bound.
A program may use at most 128 MiB of HBM per device.

```python
import math
import jax
import jax.numpy as jnp
from jax import lax

BLOCK = 64
NEIGH = 7
RIM = 32
NB_DEV = 256
PILE_DEV = 1024
TIE_DEV = 1024
NSB = 32768
PILES = 131072
GPILES = 16384
TIES = 131072
CAP = 16
PCAP = 128
N_TIE = 16
DEVICES = 128


def draw_soil_cols(key, part):
    key = jax.random.fold_in(key, 5)
    total = NB_DEV * DEVICES
    offset = jax.random.randint(key, (NEIGH, total), -RIM, RIM + 1)
    local = jnp.arange(total, dtype=jnp.int32) % NB_DEV
    row = jnp.arange(NEIGH, dtype=jnp.int32)[:, None]
    offset = jnp.where(row == 0, 0, offset)
    offset = jnp.where((row == 1) & (local == 0)[None], -RIM, offset)
    offset = jnp.where((row == NEIGH - 1) & (local == NB_DEV - 1)[None], RIM, offset)
    return (RIM + local[None] + offset).astype(jnp.int32)


def draw_tie_dest(key, part):
    key = jax.random.fold_in(key, 11)
    first, second, third = jax.random.split(key, 3)
    busiest = jax.random.randint(first, (), 0, DEVICES)
    level = jax.random.randint(second, (DEVICES, DEVICES), 0, 4)
    level = level + 8 * (jnp.arange(DEVICES)[None, :] == busiest).astype(jnp.int32)
    slot_owner = jnp.arange(DEVICES * CAP, dtype=jnp.int32) // CAP
    noise = jax.random.randint(third, (DEVICES, DEVICES * CAP), 0, 1048576)
    score = level[:, slot_owner] * 1048576 + noise
    order = jnp.argsort(-score, axis=1, stable=True)[:, :TIE_DEV]
    chosen = jnp.sort(slot_owner[order], axis=1)
    return chosen.reshape(TIES).astype(jnp.int32)


def draw_tie_pile(key, part):
    key = jax.random.fold_in(key, 17)
    first, second, third, fourth, fifth = jax.random.split(key, 5)
    busiest = jax.random.randint(first, (DEVICES,), 0, N_TIE)
    level = jax.random.randint(second, (DEVICES, N_TIE), 0, 4)
    level = level + 8 * (jnp.arange(N_TIE)[None, :] == busiest[:, None]).astype(jnp.int32)
    slot_owner = jnp.arange(N_TIE * PCAP, dtype=jnp.int32) // PCAP
    noise = jax.random.randint(third, (DEVICES, N_TIE * PCAP), 0, 1048576)
    score = level[:, slot_owner] * 1048576 + noise
    order = jnp.argsort(-score, axis=1, stable=True)[:, :TIE_DEV]
    holder = slot_owner[order]
    shuffle_keys = jax.random.randint(fourth, (DEVICES, TIE_DEV), 0, 4096) * TIE_DEV + jnp.arange(TIE_DEV, dtype=jnp.int32)[None, :]
    shuffled = jnp.argsort(shuffle_keys, axis=1)
    holder = jnp.take_along_axis(holder, shuffled, axis=1)
    segment = jax.random.randint(fifth, (DEVICES, TIE_DEV), 0, PILE_DEV)
    return (holder * PILE_DEV + segment).reshape(TIES).astype(jnp.int32)


def place_ends(drawn, stream_key, low, largest):
    longest = drawn.shape.index(max(drawn.shape))
    spots = []
    for shift in (0, 1):
        where = [jax.random.randint(jax.random.fold_in(stream_key, axis), (), 0, length) for axis, length in enumerate(drawn.shape)]
        where[longest] = (where[longest] + shift) % drawn.shape[longest]
        spots.append(tuple(where))
    return drawn.at[spots[0]].set(low).at[spots[1]].set(largest)


def block_levels(key, dims, cuts, least, high):
    loudness, own = 1.0, jax.random.fold_in(key, 6)
    for dim, blocks in cuts:
        steps = jnp.exp(jax.random.uniform(jax.random.fold_in(own, dim), (blocks,), jnp.float32, least / len(cuts), high / len(cuts)))
        loudness = loudness * jnp.repeat(steps, dims[dim] // blocks).reshape([-1 if axis == dim else 1 for axis in range(len(dims))])
    return loudness


def bell_draw(key, extent, width, reach, cuts=(), kind=jnp.bfloat16):
    values = jax.random.normal(key, extent, jnp.float32) * width
    if len(cuts) > 0:
        values = block_levels(key, extent, cuts, -0.22, 0.18) * values
    return jnp.clip(values, min=-reach, max=reach).astype(kind)


def setup_inputs(seed: int = 0) -> dict:
    splits = jax.random.split(jax.random.key(seed), 11)
    soil_disp = bell_draw(splits[0], (BLOCK, NSB), 1.0, 6.0, ((1, 128),))
    soil_vals = bell_draw(splits[1], (NEIGH, BLOCK, BLOCK, NSB), (NEIGH * BLOCK) ** -0.5, 0.25, ((3, 128),))
    soil_cols = draw_soil_cols(jax.random.fold_in(splits[10], 71), 0)
    load = bell_draw(splits[3], (BLOCK, NSB), 1.0, 6.0, ((1, 128),), jnp.float32)
    pile_disp = bell_draw(splits[4], (BLOCK, PILES), 1.0, 6.0, ((1, 128),))
    tie_vals = bell_draw(splits[5], (BLOCK, BLOCK, TIES), BLOCK ** -0.5, 0.75, ((2, 128),))
    tie_pile = draw_tie_pile(jax.random.fold_in(splits[10], 71), 0)
    tie_limit = jnp.clip(jnp.exp(math.log(3.0) - 2.3025851 * jax.random.uniform(splits[7], (TIES,), jnp.float32) ** block_levels(splits[7], (TIES,), ((0, 128),), -0.2, 0.2)), 0.3, 3.0)
    tie_dest = draw_tie_dest(jax.random.fold_in(splits[10], 71), 0)
    tie_block = place_ends(jax.random.randint(splits[9], (TIES,), 0, NB_DEV), jax.random.fold_in(splits[9], 1), 0, NB_DEV - 1).astype(jnp.int32)
    return {"soil_disp": soil_disp, "soil_vals": soil_vals, "soil_cols": soil_cols, "load": load, "pile_disp": pile_disp, "tie_vals": tie_vals, "tie_pile": tie_pile, "tie_limit": tie_limit, "tie_dest": tie_dest, "tie_block": tie_block}


def reference(soil_disp, soil_vals, soil_cols, load, pile_disp, tie_vals, tie_pile, tie_limit, tie_dest, tie_block):
    disp = soil_disp.astype(jnp.float32)
    piles = pile_disp.astype(jnp.float32)

    def one_device(device):
        base = device * NB_DEV
        values = lax.dynamic_slice_in_dim(soil_vals, base, NB_DEV, 3).astype(jnp.float32)
        columns = lax.dynamic_slice_in_dim(soil_cols, base, NB_DEV, 1)
        global_cols = base + columns - RIM
        inside = ((global_cols >= 0) & (global_cols < NSB)).astype(jnp.float32)
        picked = disp[:, jnp.clip(global_cols, 0, NSB - 1)] * inside[None]
        image = jnp.einsum('kijb,jkb->ib', values, picked)
        tie_base = device * TIE_DEV
        blocks = lax.dynamic_slice_in_dim(tie_vals, tie_base, TIE_DEV, 2).astype(jnp.float32)
        local_pile = lax.dynamic_slice_in_dim(tie_pile, tie_base, TIE_DEV, 0)
        pile_index = (device // N_TIE * GPILES + local_pile).astype(jnp.int32)
        gap = jnp.einsum('ijt,jt->it', blocks, piles[:, pile_index])
        limit = lax.dynamic_slice_in_dim(tie_limit, tie_base, TIE_DEV, 0)
        ratio = gap / limit[None]
        force = (gap / jnp.sqrt(1.0 + ratio * ratio)).astype(jnp.bfloat16)
        return (image, force)
    images, forces = lax.map(one_device, jnp.arange(DEVICES, dtype=jnp.int32))
    soil_image = jnp.transpose(images, (1, 0, 2)).reshape(BLOCK, NSB)
    force_all = jnp.transpose(forces, (1, 0, 2)).reshape(BLOCK, TIES)
    target = (tie_dest * NB_DEV + tie_block).astype(jnp.int32)
    tie_total = jnp.zeros((BLOCK, NSB), jnp.float32).at[:, target].add(force_all.astype(jnp.float32))
    return soil_image + tie_total - load
```

```python
import jax
import jax.numpy as jnp
from jax import lax
from jax.experimental import pallas as pl
from jax.experimental.pallas import tpu as pltpu
from jax.sharding import PartitionSpec as P

MESH = pl.DeviceIdType.MESH
F32, BF16, I32 = jnp.float32, jnp.bfloat16, jnp.int32
NT, NG = 16, 8
ND = NT * NG
PCAP, CAP = 128, 16
B = 64
T = 1024
L = 128
NC = T // L


def one_hot(cond):
    return jnp.where(cond, 1.0, 0.0).astype(BF16)


def iota(shape, dim):
    return lax.broadcasted_iota(I32, shape, dim)


def slots(ids, n, cap):
    before = iota((L, 2 * L), 0)
    now = iota((L, 2 * L), 1)
    tri = one_hot((before < now) | (now >= L))
    rows = [ids[c : c + 1, :] == iota((n, L), 0) for c in range(NC)]
    hot = jnp.concatenate([one_hot(r) for r in rows], axis=0)
    sums = jnp.dot(hot, tri, preferred_element_type=F32)
    run = jnp.zeros((n, L), F32)
    out = []
    for c in range(NC):
        part = sums[c * n : (c + 1) * n]
        rank = jnp.sum(jnp.where(rows[c], part[:, :L] + run, 0.0), axis=0, keepdims=True)
        out.append(ids[c : c + 1, :] * cap + rank.astype(I32))
        run = run + part[:, L:]
    return out


def kernel(
    soil_disp, soil_vals, soil_cols, load, pile_disp, tie_vals, tie_pile, tie_limit, tie_dest, tie_block,
    out,
    sd, sv, sc, ld, pd, tv, tp, tl, td, tb,
    hot_p, hot_d, ask, asked, answer, piles, state, force, send, got, rim, acc, image,
    in_sem, ask_s, ask_r, ans_s, ans_r, rim_s, rim_r, frc_s, frc_r, ready,
):
    g, t = lax.axis_index("grp"), lax.axis_index("tie")
    me = g * NT + t
    bar = pltpu.get_barrier_semaphore()

    def greet_tie(k, _):
        pl.semaphore_signal(bar, inc=1, device_id=(g, lax.rem(t + k, NT)), device_id_type=MESH)
        return 0

    def greet_grp(k, _):
        pl.semaphore_signal(bar, inc=1, device_id=(lax.rem(g + k, NG), t), device_id_type=MESH)
        return 0

    lax.fori_loop(1, NT, greet_tie, 0)
    lax.fori_loop(1, NG, greet_grp, 0)

    pairs = [
        (tie_pile, tp), (pile_disp, pd), (tie_dest, td), (tie_block, tb), (tie_limit, tl), (soil_disp, sd),
        (soil_cols, sc), (load, ld), (tie_vals, tv), (soil_vals, sv),
    ]
    loads = {}
    for n, (src, dst) in enumerate(pairs):
        copy = pltpu.make_async_copy(src, dst, in_sem.at[n])
        copy.start()
        loads[n] = copy

    loads[0].wait()
    ids = tp[...]
    holder = ids // T
    seg = ids - holder * T
    where = slots(holder, NT, PCAP)

    def fill_p(h, _):
        for c in range(NC):
            hot_p[h, :, c * L : (c + 1) * L] = one_hot((where[c] - h * PCAP) == iota((PCAP, L), 0))
        return 0

    lax.fori_loop(0, NT, fill_p, 0)
    hi = seg // 32
    lo = seg - hi * 32
    hi_row = jnp.concatenate([hi[c : c + 1, :] for c in range(NC)], axis=1).astype(F32)
    lo_row = jnp.concatenate([lo[c : c + 1, :] for c in range(NC)], axis=1).astype(F32)
    first = iota((16, T), 0)
    digits = jnp.where(first == 0, hi_row, jnp.where(first == 1, lo_row, 0.0)).astype(BF16)

    def fill_ask(q, _):
        named = lax.dot_general(
            digits, hot_p[pl.ds(q * 4, 4)].reshape(4 * PCAP, T), (((1,), (1,)), ((), ())), preferred_element_type=F32
        )
        number = (named[0:1] * 32.0 + named[1:2]).astype(I32)
        for h in range(4):
            ask[q * 4 + h] = jnp.broadcast_to(number[:, h * L : (h + 1) * L], (8, L))
        return 0

    lax.fori_loop(0, NT // 4, fill_ask, 0)

    pl.semaphore_wait(bar, NT - 1 + NG - 1)

    def ask_copy(k):
        h = lax.rem(t + k, NT)
        return pltpu.make_async_remote_copy(
            ask.at[h], asked.at[t], ask_s.at[k], ask_r.at[k], device_id=(g, h), device_id_type=MESH
        )

    def start_ask(k, _):
        ask_copy(k).start()
        return 0

    lax.fori_loop(1, NT, start_ask, 0)
    asked[t] = ask[t]

    def greet_again(k, _):
        pl.semaphore_signal(ready, inc=1, device_id=(lax.rem(g + k, NG), t), device_id_type=MESH)
        return 0

    lax.fori_loop(1, NG, greet_again, 0)

    loads[2].wait()
    goes = slots(td[...], ND, CAP)

    def fill_d(m, _):
        for c in range(NC):
            hot_d[pl.ds(m * L, L), c * L : (c + 1) * L] = one_hot((goes[c] - m * L) == iota((L, L), 0))
        return 0

    lax.fori_loop(0, ND * CAP // L, fill_d, 0)

    loads[1].wait()

    def wait_ask(k, _):
        ask_copy(k).wait()
        return 0

    lax.fori_loop(1, NT, wait_ask, 0)

    def answer_copy(k):
        r = lax.rem(t + k, NT)
        return pltpu.make_async_remote_copy(
            answer.at[r], piles.at[t], ans_s.at[k], ans_r.at[k], device_id=(g, r), device_id_type=MESH
        )

    for q in range(NT // 4):
        hots = []
        for n in range(4):
            r = lax.rem(t + q * 4 + n + 1, NT)
            hots.append(one_hot(asked[r][0:1, :] == iota((T, L), 0)))
        found = jnp.dot(pd[...], jnp.concatenate(hots, axis=1), preferred_element_type=F32).astype(BF16)
        for n in range(4):
            k = q * 4 + n + 1
            block = found[:, n * L : (n + 1) * L]
            if k < NT:
                answer[lax.rem(t + k, NT)] = block
                answer_copy(k).start()
            else:
                piles[t] = block

    pl.semaphore_wait(ready, NG - 1)
    loads[5].wait()
    right, left = lax.rem(me + 1, ND), lax.rem(me + ND - 1, ND)
    to_right = pltpu.make_async_remote_copy(
        sd.at[:, pl.ds(L, L)], rim.at[0], rim_s.at[0], rim_r.at[0],
        device_id=(right // NT, lax.rem(right, NT)), device_id_type=MESH,
    )
    to_left = pltpu.make_async_remote_copy(
        sd.at[:, pl.ds(0, L)], rim.at[1], rim_s.at[1], rim_r.at[1],
        device_id=(left // NT, lax.rem(left, NT)), device_id_type=MESH,
    )
    to_right.start()
    to_left.start()

    for q in range(NT // 4):
        for n in range(4):
            if q * 4 + n > 0:
                answer_copy(q * 4 + n).wait()
        held = [lax.rem(t + NT - (q * 4 + n), NT) for n in range(4)]
        left_side = jnp.concatenate([piles[h] for h in held], axis=1)
        right_side = jnp.concatenate([hot_p[h] for h in held], axis=0)
        part = jnp.dot(left_side, right_side, preferred_element_type=F32)
        state[...] = part if q == 0 else state[...] + part

    for n in (3, 4, 8):
        loads[n].wait()
    force[B:] = jnp.zeros((L - B, T), BF16)
    for c in range(NC):
        cols = slice(c * L, (c + 1) * L)
        x = state[:, cols]
        limit = tl[c : c + 1, :]

        def rows(i, _):
            at = pl.multiple_of(i * 16, 16)
            y = tv[pl.ds(at, 16), :, cols].astype(F32) * x[None]
            gap = jnp.sum(jnp.sum(y.reshape(16, 8, 8, L), axis=1), axis=1)
            ratio = gap / limit
            force[pl.ds(at, 16), cols] = (gap / jnp.sqrt(1.0 + ratio * ratio)).astype(BF16)
            return 0

        lax.fori_loop(0, B // 16, rows, 0)
        tail = jnp.where(iota((16, L), 0) == 0, tb[c : c + 1, :].astype(F32), 0.0)
        force[B : B + 16, cols] = tail.astype(BF16)

    for m, (low, high) in enumerate(((0, 512), (0, T), (0, T), (512, T))):
        packed = lax.dot_general(
            hot_d[m * 512 : (m + 1) * 512, low:high], force[:, low:high], (((1,), (1,)), ((), ())),
            preferred_element_type=F32,
        )
        send[m * 512 : (m + 1) * 512] = packed.astype(BF16)

    def force_copy(k):
        d = lax.rem(me + k, ND)
        return pltpu.make_async_remote_copy(
            send.at[pl.ds(pl.multiple_of(d * CAP, CAP), CAP)], got.at[pl.ds(pl.multiple_of(me * CAP, CAP), CAP)],
            frc_s, frc_r, device_id=(d // NT, lax.rem(d, NT)), device_id_type=MESH,
        )

    def start_force(k, _):
        force_copy(k).start()
        return 0

    lax.fori_loop(1, ND, start_force, 0)
    own = pl.ds(pl.multiple_of(me * CAP, CAP), CAP)
    got[own] = send[own]

    loads[6].wait()
    to_right.wait()
    to_left.wait()
    before = jnp.where(me == 0, 0.0, rim[0].astype(F32)).astype(BF16)
    after = jnp.where(me == ND - 1, 0.0, rim[1].astype(F32)).astype(BF16)
    wide = jnp.concatenate([before, sd[...], after], axis=1)
    loads[9].wait()
    for c in range(2):
        cols = slice(c * L, (c + 1) * L)
        near = wide[:, c * L : c * L + 3 * L]
        acc[...] = jnp.zeros_like(acc)
        for k in range(7):
            at = sc[k : k + 1, cols] + (96 - c * L)
            x = jnp.dot(near, one_hot(at == iota((3 * L, L), 0)), preferred_element_type=F32)

            def more(i, _, k=k, x=x, cols=cols):
                rows = pl.ds(pl.multiple_of(i * 16, 16), 16)
                y = sv[k, rows, :, cols].astype(F32) * x[None]
                acc[rows] = acc[rows] + jnp.sum(y.reshape(16, 8, 8, L), axis=1)
                return 0

            lax.fori_loop(0, B // 16, more, 0)
        image[:, cols] = jnp.sum(acc[...], axis=1)

    n = (ND - 1) * CAP
    pltpu.make_async_remote_copy(
        send.at[pl.ds(0, n)], got.at[pl.ds(0, n)], frc_s, frc_r, device_id=(g, t), device_id_type=MESH
    ).wait()
    loads[7].wait()
    block = got[:, B : B + 1].astype(F32).astype(I32)
    spread = one_hot(block == iota((ND * CAP, 256), 1))
    total = lax.dot_general(got[...], spread, (((0,), (0,)), ((), ())), preferred_element_type=F32)
    out[...] = image[...] + total[:B] - ld[...]


def on_device(
    soil_disp, soil_vals, soil_cols, load, pile_disp, tie_vals, tie_pile, tie_limit, tie_dest, tie_block
):
    lanes = [x.reshape(NC, L) for x in (tie_pile, tie_limit, tie_dest, tie_block)]
    args = [soil_disp, soil_vals, soil_cols, load, pile_disp, tie_vals, *lanes]
    dma = pltpu.SemaphoreType.DMA
    return pl.pallas_call(
        kernel,
        out_shape=jax.ShapeDtypeStruct(load.shape, F32),
        in_specs=[pl.BlockSpec(memory_space=pl.ANY)] * len(args),
        out_specs=pl.BlockSpec(memory_space=pltpu.VMEM),
        scratch_shapes=[
            *[pltpu.VMEM(x.shape, x.dtype) for x in args],
            pltpu.VMEM((NT, PCAP, T), BF16),
            pltpu.VMEM((ND * CAP, T), BF16),
            pltpu.VMEM((NT, 8, L), I32),
            pltpu.VMEM((NT, 8, L), I32),
            pltpu.VMEM((NT, B, L), BF16),
            pltpu.VMEM((NT, B, L), BF16),
            pltpu.VMEM((B, T), F32),
            pltpu.VMEM((L, T), BF16),
            pltpu.VMEM((ND * CAP, L), BF16),
            pltpu.VMEM((ND * CAP, L), BF16),
            pltpu.VMEM((2, B, L), BF16),
            pltpu.VMEM((B, 8, L), F32),
            pltpu.VMEM((B, 256), F32),
            dma((len(args),)),
            dma((NT,)), dma((NT,)), dma((NT,)), dma((NT,)), dma((2,)), dma((2,)), dma, dma,
            pltpu.SemaphoreType.REGULAR,
        ],
        compiler_params=pltpu.CompilerParams(
            collective_id=0, has_side_effects=True, vmem_limit_bytes=56 * 1024 * 1024
        ),
        cost_estimate=pl.CostEstimate(flops=3_000_000_000, bytes_accessed=24_000_000, transcendentals=65536),
        name="residual",
    )(*args)


def solution(mesh):
    both = ("grp", "tie")
    return jax.shard_map(
        on_device,
        mesh=mesh,
        in_specs=(
            P(None, both), P(None, None, None, both), P(None, both), P(None, both), P(None, both),
            P(None, None, both), P(both), P(both), P(both), P(both),
        ),
        out_specs=P(None, both),
        check_vma=False,
    )
```

```python
import jax
import jax.numpy as jnp
from jax import lax
from jax.experimental import pallas as pl
from jax.experimental.pallas import tpu as pltpu
from jax.sharding import PartitionSpec as P

MESH = pl.DeviceIdType.MESH
F32, BF16, I32 = jnp.float32, jnp.bfloat16, jnp.int32
NT, NG = 16, 8
ND = NT * NG
PCAP, CAP = 128, 16
B = 64
T = 1024
L = 128
NC = T // L


def one_hot(cond):
    return jnp.where(cond, 1.0, 0.0).astype(BF16)


def iota(shape, dim):
    return lax.broadcasted_iota(I32, shape, dim)


def slots(ids, n, cap):
    before = iota((L, 2 * L), 0)
    now = iota((L, 2 * L), 1)
    tri = one_hot((before < now) | (now >= L))
    rows = [ids[c : c + 1, :] == iota((n, L), 0) for c in range(NC)]
    hot = jnp.concatenate([one_hot(r) for r in rows], axis=0)
    sums = jnp.dot(hot, tri, preferred_element_type=F32)
    run = jnp.zeros((n, L), F32)
    out = []
    for c in range(NC):
        part = sums[c * n : (c + 1) * n]
        rank = jnp.sum(jnp.where(rows[c], part[:, :L] + run, 0.0), axis=0, keepdims=True)
        out.append(ids[c : c + 1, :] * cap + rank.astype(I32))
        run = run + part[:, L:]
    return out


def kernel(
    soil_disp, soil_vals, soil_cols, load, pile_disp, tie_vals, tie_pile, tie_limit, tie_dest, tie_block,
    out,
    sd, sv, sc, ld, pd, tv, tp, tl, td, tb,
    hot_p, hot_d, ask, asked, answer, piles, state, force, slotted, send, got, rim, acc, image,
    in_sem, ask_s, ask_r, ans_s, ans_r, rim_s, rim_r, frc_s, frc_r, ready,
):
    g, t = lax.axis_index("grp"), lax.axis_index("tie")
    me = g * NT + t
    bar = pltpu.get_barrier_semaphore()

    def greet_tie(k, _):
        pl.semaphore_signal(bar, inc=1, device_id=(g, lax.rem(t + k, NT)), device_id_type=MESH)
        return 0

    def greet_grp(k, _):
        pl.semaphore_signal(bar, inc=1, device_id=(lax.rem(g + k, NG), t), device_id_type=MESH)
        return 0

    lax.fori_loop(1, NT, greet_tie, 0)
    lax.fori_loop(1, NG, greet_grp, 0)

    pairs = [
        (tie_pile, tp), (pile_disp, pd), (tie_dest, td), (tie_block, tb), (tie_limit, tl), (soil_disp, sd),
        (soil_cols, sc), (load, ld),
    ]
    pairs += [(tie_vals.at[:, :, pl.ds(c * L, L)], tv.at[c]) for c in range(NC)]
    pairs += [(soil_vals.at[:, :, :, pl.ds(c * L, L)], sv.at[c]) for c in range(2)]
    loads = {}
    for n, (src, dst) in enumerate(pairs):
        copy = pltpu.make_async_copy(src, dst, in_sem.at[n])
        copy.start()
        loads[n] = copy

    loads[0].wait()
    ids = tp[...]
    holder = ids // T
    seg = ids - holder * T
    where = slots(holder, NT, PCAP)

    def fill_p(h, _):
        for c in range(NC):
            hot_p[h, :, c * L : (c + 1) * L] = one_hot((where[c] - h * PCAP) == iota((PCAP, L), 0))
        return 0

    lax.fori_loop(0, NT, fill_p, 0)
    hi = seg // 32
    lo = seg - hi * 32
    hi_row = jnp.concatenate([hi[c : c + 1, :] for c in range(NC)], axis=1).astype(F32)
    lo_row = jnp.concatenate([lo[c : c + 1, :] for c in range(NC)], axis=1).astype(F32)
    first = iota((16, T), 0)
    digits = jnp.where(first == 0, hi_row, jnp.where(first == 1, lo_row, 0.0)).astype(BF16)

    def fill_ask(q, _):
        named = lax.dot_general(
            digits, hot_p[pl.ds(q * 4, 4)].reshape(4 * PCAP, T), (((1,), (1,)), ((), ())), preferred_element_type=F32
        )
        number = (named[0:1] * 32.0 + named[1:2]).astype(I32)
        for h in range(4):
            ask[q * 4 + h] = number[:, h * L : (h + 1) * L]
        return 0

    lax.fori_loop(0, NT // 4, fill_ask, 0)

    pl.semaphore_wait(bar, NT - 1 + NG - 1)

    def ask_copy(k):
        h = lax.rem(t + k, NT)
        return pltpu.make_async_remote_copy(
            ask.at[h], asked.at[t], ask_s.at[k], ask_r.at[k], device_id=(g, h), device_id_type=MESH
        )

    def start_ask(k, _):
        ask_copy(k).start()
        return 0

    lax.fori_loop(1, NT, start_ask, 0)
    asked[t] = ask[t]

    def greet_again(k, _):
        pl.semaphore_signal(ready, inc=1, device_id=(lax.rem(g + k, NG), t), device_id_type=MESH)
        return 0

    lax.fori_loop(1, NG, greet_again, 0)

    loads[2].wait()
    goes = slots(td[...], ND, CAP)

    def fill_d(m, _):
        for c in range(NC):
            hot_d[pl.ds(m * L, L), c * L : (c + 1) * L] = one_hot((goes[c] - m * L) == iota((L, L), 0))
        return 0

    lax.fori_loop(0, ND * CAP // L, fill_d, 0)

    loads[1].wait()

    def answer_copy(k):
        r = lax.rem(t + k, NT)
        return pltpu.make_async_remote_copy(
            answer.at[r], piles.at[t], ans_s.at[k], ans_r.at[k], device_id=(g, r), device_id_type=MESH
        )

    for q in range(NT // 4):
        hots = []
        for n in range(4):
            if q * 4 + n + 1 < NT:
                ask_copy(NT - (q * 4 + n + 1)).wait()
            r = lax.rem(t + q * 4 + n + 1, NT)
            hots.append(one_hot(asked[r] == iota((T, L), 0)))
        found = jnp.dot(pd[...], jnp.concatenate(hots, axis=1), preferred_element_type=F32).astype(BF16)
        for n in range(4):
            k = q * 4 + n + 1
            block = found[:, n * L : (n + 1) * L]
            if k < NT:
                answer[lax.rem(t + k, NT)] = block
                answer_copy(k).start()
            else:
                piles[t] = block

    pl.semaphore_wait(ready, NG - 1)
    loads[5].wait()
    right, left = lax.rem(me + 1, ND), lax.rem(me + ND - 1, ND)
    to_right = pltpu.make_async_remote_copy(
        sd.at[:, pl.ds(L, L)], rim.at[0], rim_s.at[0], rim_r.at[0],
        device_id=(right // NT, lax.rem(right, NT)), device_id_type=MESH,
    )
    to_left = pltpu.make_async_remote_copy(
        sd.at[:, pl.ds(0, L)], rim.at[1], rim_s.at[1], rim_r.at[1],
        device_id=(left // NT, lax.rem(left, NT)), device_id_type=MESH,
    )
    to_right.start()
    to_left.start()

    for q in range(NT // 4):
        for n in range(4):
            if q * 4 + n > 0:
                answer_copy(q * 4 + n).wait()
        held = [lax.rem(t + NT - (q * 4 + n), NT) for n in range(4)]
        left_side = jnp.concatenate([piles[h] for h in held], axis=1)
        right_side = jnp.concatenate([hot_p[h] for h in held], axis=0)
        part = jnp.dot(left_side, right_side, preferred_element_type=F32)
        state[...] = part if q == 0 else state[...] + part

    loads[3].wait()
    loads[4].wait()
    for c in range(NC):
        cols = slice(c * L, (c + 1) * L)
        x = state[:, cols].astype(BF16)
        loads[8 + c].wait()
        for i in range(0, B, 16):
            y = tv[c, i : i + 16] * x[None]
            y = (y[:, :32] + y[:, 32:]).astype(F32)
            gap = jnp.sum(jnp.sum(y.reshape(16, 4, 8, L), axis=1), axis=1)
            ratio = gap / tl[c : c + 1, :]
            force[i : i + 16, cols] = (gap / jnp.sqrt(1.0 + ratio * ratio)).astype(BF16)
        tail = jnp.where(iota((B, L), 0) == 0, tb[c : c + 1, :].astype(F32), 0.0)
        force[B:, cols] = tail.astype(BF16)
        if c % 2:
            low = (c - 1) * L
            pair = slice(low, low + 2 * L)
            packed = lax.dot_general(
                hot_d[low : low + T + 2 * L, pair], force[:, pair], (((1,), (1,)), ((), ())), preferred_element_type=F32
            )
            if c == 1:
                slotted[: T + 2 * L] = packed
            else:
                slotted[low : low + T] = slotted[low : low + T] + packed[:T]
                slotted[low + T : low + T + 2 * L] = packed[T:]
    for m in range(0, ND * CAP, 512):
        send[m : m + 512] = slotted[m : m + 512].astype(BF16)

    def force_copy(k):
        d = lax.rem(me + k, ND)
        return pltpu.make_async_remote_copy(
            send.at[pl.ds(pl.multiple_of(d * CAP, CAP), CAP)], got.at[pl.ds(pl.multiple_of(me * CAP, CAP), CAP)],
            frc_s, frc_r, device_id=(d // NT, lax.rem(d, NT)), device_id_type=MESH,
        )

    def start_force(k, _):
        force_copy(k).start()
        return 0

    lax.fori_loop(1, ND, start_force, 0)
    own = pl.ds(pl.multiple_of(me * CAP, CAP), CAP)
    got[own] = send[own]

    loads[6].wait()
    to_right.wait()
    to_left.wait()
    before = jnp.where(me == 0, 0.0, rim[0].astype(F32)).astype(BF16)
    after = jnp.where(me == ND - 1, 0.0, rim[1].astype(F32)).astype(BF16)
    wide = jnp.concatenate([before, sd[...], after], axis=1)
    for c in range(2):
        loads[8 + NC + c].wait()
        cols = slice(c * L, (c + 1) * L)
        near = wide[:, c * L : c * L + 3 * L]
        acc[...] = jnp.zeros_like(acc)
        for k in range(7):
            at = sc[k : k + 1, cols] + (96 - c * L)
            x = jnp.dot(near, one_hot(at == iota((3 * L, L), 0)), preferred_element_type=F32)

            def more(i, _, c=c, k=k, x=x):
                rows = pl.ds(pl.multiple_of(i * 16, 16), 16)
                y = sv[c, k, rows].astype(F32) * x[None]
                acc[rows] = acc[rows] + jnp.sum(y.reshape(16, 8, 8, L), axis=1)
                return 0

            lax.fori_loop(0, B // 16, more, 0)
        image[:, cols] = jnp.sum(acc[...], axis=1)

    n = (ND - 1) * CAP
    pltpu.make_async_remote_copy(
        send.at[pl.ds(0, n)], got.at[pl.ds(0, n)], frc_s, frc_r, device_id=(g, t), device_id_type=MESH
    ).wait()
    loads[7].wait()
    block = got[:, B : B + 1].astype(F32).astype(I32)
    spread = one_hot(block == iota((ND * CAP, 256), 1))
    total = lax.dot_general(got[...], spread, (((0,), (0,)), ((), ())), preferred_element_type=F32)
    out[...] = image[...] + total[:B] - ld[...]


def on_device(
    soil_disp, soil_vals, soil_cols, load, pile_disp, tie_vals, tie_pile, tie_limit, tie_dest, tie_block
):
    lanes = [x.reshape(NC, L) for x in (tie_pile, tie_limit, tie_dest, tie_block)]
    args = [soil_disp, soil_vals, soil_cols, load, pile_disp, tie_vals, *lanes]
    tiles = {1: (2, 7, B, B, L), 5: (NC, B, B, L)}
    dma = pltpu.SemaphoreType.DMA
    return pl.pallas_call(
        kernel,
        out_shape=jax.ShapeDtypeStruct(load.shape, F32),
        in_specs=[pl.BlockSpec(memory_space=pl.ANY)] * len(args),
        out_specs=pl.BlockSpec(memory_space=pltpu.VMEM),
        scratch_shapes=[
            *[pltpu.VMEM(tiles.get(n, x.shape), x.dtype) for n, x in enumerate(args)],
            pltpu.VMEM((NT, PCAP, T), BF16),
            pltpu.VMEM((ND * CAP, T), BF16),
            pltpu.VMEM((NT, 1, L), I32),
            pltpu.VMEM((NT, 1, L), I32),
            pltpu.VMEM((NT, B, L), BF16),
            pltpu.VMEM((NT, B, L), BF16),
            pltpu.VMEM((B, T), F32),
            pltpu.VMEM((L, T), BF16),
            pltpu.VMEM((ND * CAP, L), F32),
            pltpu.VMEM((ND * CAP, L), BF16),
            pltpu.VMEM((ND * CAP, L), BF16),
            pltpu.VMEM((2, B, L), BF16),
            pltpu.VMEM((B, 8, L), F32),
            pltpu.VMEM((B, 256), F32),
            dma((8 + NC + 2,)),
            dma((NT,)), dma((NT,)), dma((NT,)), dma((NT,)), dma((2,)), dma((2,)), dma, dma,
            pltpu.SemaphoreType.REGULAR,
        ],
        compiler_params=pltpu.CompilerParams(
            collective_id=0, has_side_effects=True, vmem_limit_bytes=56 * 1024 * 1024
        ),
        cost_estimate=pl.CostEstimate(flops=3_000_000_000, bytes_accessed=24_000_000, transcendentals=65536),
        name="residual",
    )(*args)


def solution(mesh):
    both = ("grp", "tie")
    return jax.shard_map(
        on_device,
        mesh=mesh,
        in_specs=(
            P(None, both), P(None, None, None, both), P(None, both), P(None, both), P(None, both),
            P(None, None, both), P(both), P(both), P(both), P(both),
        ),
        out_specs=P(None, both),
        check_vma=False,
    )
```

```python
import jax
import jax.numpy as jnp
from jax import lax
from jax.experimental import pallas as pl
from jax.experimental.pallas import tpu as pltpu
from jax.sharding import PartitionSpec as P

MESH = pl.DeviceIdType.MESH
F32, BF16, I32 = jnp.float32, jnp.bfloat16, jnp.int32
NT, NG = 16, 8
ND = NT * NG
PCAP, CAP = 128, 16
B = 64
T = 1024
L = 128
NC = T // L


def one_hot(cond):
    return jnp.where(cond, 1.0, 0.0).astype(BF16)


def iota(shape, dim):
    return lax.broadcasted_iota(I32, shape, dim)


def slots(ids, n, cap):
    before = iota((L, 2 * L), 0)
    now = iota((L, 2 * L), 1)
    tri = one_hot((before < now) | (now >= L))
    rows = [ids[c : c + 1, :] == iota((n, L), 0) for c in range(NC)]
    hot = jnp.concatenate([one_hot(r) for r in rows], axis=0)
    sums = jnp.dot(hot, tri, preferred_element_type=F32)
    run = jnp.zeros((n, L), F32)
    out = []
    for c in range(NC):
        part = sums[c * n : (c + 1) * n]
        rank = jnp.sum(jnp.where(rows[c], part[:, :L] + run, 0.0), axis=0, keepdims=True)
        out.append(ids[c : c + 1, :] * cap + rank.astype(I32))
        run = run + part[:, L:]
    return out


def kernel(
    soil_disp, soil_vals, soil_cols, load, pile_disp, tie_vals, tie_pile, tie_limit, tie_dest, tie_block,
    out,
    sd, sv, sc, ld, pd, tv, tp, tl, td, tb,
    hot_p, hot_d, ask, asked, answer, piles, state, force, slotted, send, got, rim, acc, image,
    in_sem, ask_s, ask_r, ans_s, ans_r, rim_s, rim_r, frc_s, frc_r, ready,
):
    g, t = lax.axis_index("grp"), lax.axis_index("tie")
    me = g * NT + t
    bar = pltpu.get_barrier_semaphore()

    def greet_tie(k, _):
        pl.semaphore_signal(bar, inc=1, device_id=(g, lax.rem(t + k, NT)), device_id_type=MESH)
        return 0

    def greet_grp(k, _):
        pl.semaphore_signal(bar, inc=1, device_id=(lax.rem(g + k, NG), t), device_id_type=MESH)
        return 0

    lax.fori_loop(1, NT, greet_tie, 0)
    lax.fori_loop(1, NG, greet_grp, 0)

    pairs = [
        (tie_pile, tp), (pile_disp, pd), (tie_dest, td), (tie_block, tb), (tie_limit, tl), (soil_disp, sd),
        (soil_cols, sc), (load, ld),
    ]
    pairs += [(tie_vals.at[:, :, pl.ds(c * L, L)], tv.at[c]) for c in range(NC)]
    pairs += [(soil_vals.at[:, :, :, pl.ds(c * L, L)], sv.at[c]) for c in range(2)]
    loads = {}
    for n, (src, dst) in enumerate(pairs):
        copy = pltpu.make_async_copy(src, dst, in_sem.at[n])
        copy.start()
        loads[n] = copy

    loads[0].wait()
    ids = tp[...]
    holder = ids // T
    seg = ids - holder * T
    where = slots(holder, NT, PCAP)

    def fill_p(h, _):
        for c in range(NC):
            hot_p[h, :, c * L : (c + 1) * L] = one_hot((where[c] - h * PCAP) == iota((PCAP, L), 0))
        return 0

    lax.fori_loop(0, NT, fill_p, 0)
    hi = seg // 32
    lo = seg - hi * 32
    hi_row = jnp.concatenate([hi[c : c + 1, :] for c in range(NC)], axis=1).astype(F32)
    lo_row = jnp.concatenate([lo[c : c + 1, :] for c in range(NC)], axis=1).astype(F32)
    first = iota((16, T), 0)
    digits = jnp.where(first == 0, hi_row, jnp.where(first == 1, lo_row, 0.0)).astype(BF16)

    def fill_ask(q, _):
        named = lax.dot_general(
            digits, hot_p[pl.ds(q * 4, 4)].reshape(4 * PCAP, T), (((1,), (1,)), ((), ())), preferred_element_type=F32
        )
        number = (named[0:1] * 32.0 + named[1:2]).astype(I32)
        for h in range(4):
            ask[q * 4 + h] = number[:, h * L : (h + 1) * L]
        return 0

    lax.fori_loop(0, NT // 4, fill_ask, 0)

    pl.semaphore_wait(bar, NT - 1 + NG - 1)

    def ask_copy(k):
        h = lax.rem(t + k, NT)
        return pltpu.make_async_remote_copy(
            ask.at[h], asked.at[t], ask_s.at[k], ask_r.at[k], device_id=(g, h), device_id_type=MESH
        )

    def start_ask(k, _):
        ask_copy(k).start()
        return 0

    lax.fori_loop(1, NT, start_ask, 0)
    asked[t] = ask[t]

    def greet_again(k, _):
        pl.semaphore_signal(ready, inc=1, device_id=(lax.rem(g + k, NG), t), device_id_type=MESH)
        return 0

    lax.fori_loop(1, NG, greet_again, 0)

    loads[2].wait()
    goes = slots(td[...], ND, CAP)

    def fill_d(m, _):
        for c in range(NC):
            hot_d[pl.ds(m * L, L), c * L : (c + 1) * L] = one_hot((goes[c] - m * L) == iota((L, L), 0))
        return 0

    lax.fori_loop(0, ND * CAP // L, fill_d, 0)

    loads[1].wait()

    def answer_copy(k):
        r = lax.rem(t + k, NT)
        return pltpu.make_async_remote_copy(
            answer.at[r], piles.at[t], ans_s.at[k], ans_r.at[k], device_id=(g, r), device_id_type=MESH
        )

    for q in range(NT // 4):
        hots = []
        for n in range(4):
            if q * 4 + n + 1 < NT:
                ask_copy(NT - (q * 4 + n + 1)).wait()
            r = lax.rem(t + q * 4 + n + 1, NT)
            hots.append(one_hot(asked[r] == iota((T, L), 0)))
        found = jnp.dot(pd[...], jnp.concatenate(hots, axis=1), preferred_element_type=F32).astype(BF16)
        for n in range(4):
            k = q * 4 + n + 1
            block = found[:, n * L : (n + 1) * L]
            if k < NT:
                answer[lax.rem(t + k, NT)] = block
                answer_copy(k).start()
            else:
                piles[t] = block

    pl.semaphore_wait(ready, NG - 1)
    loads[5].wait()
    right, left = lax.rem(me + 1, ND), lax.rem(me + ND - 1, ND)
    to_right = pltpu.make_async_remote_copy(
        sd.at[:, pl.ds(L, L)], rim.at[0], rim_s.at[0], rim_r.at[0],
        device_id=(right // NT, lax.rem(right, NT)), device_id_type=MESH,
    )
    to_left = pltpu.make_async_remote_copy(
        sd.at[:, pl.ds(0, L)], rim.at[1], rim_s.at[1], rim_r.at[1],
        device_id=(left // NT, lax.rem(left, NT)), device_id_type=MESH,
    )
    to_right.start()
    to_left.start()

    for q in range(NT // 4):
        for n in range(4):
            if q * 4 + n > 0:
                answer_copy(q * 4 + n).wait()
        held = [lax.rem(t + NT - (q * 4 + n), NT) for n in range(4)]
        left_side = jnp.concatenate([piles[h] for h in held], axis=1)
        right_side = jnp.concatenate([hot_p[h] for h in held], axis=0)
        part = jnp.dot(left_side, right_side, preferred_element_type=F32)
        state[...] = part if q == 0 else state[...] + part

    loads[3].wait()
    loads[4].wait()
    slotted[...] = jnp.zeros_like(slotted)
    force[B:] = jnp.zeros((B, T), BF16)
    for c in range(NC):
        force[B : B + 16, c * L : (c + 1) * L] = jnp.where(
            iota((16, L), 0) == 0, tb[c : c + 1, :].astype(F32), 0.0
        ).astype(BF16)
        loads[8 + c].wait()

    def two_columns(p, _):
        for n in range(2):
            c = p * 2 + n
            cols = pl.ds(pl.multiple_of(c * L, L), L)
            x = state[:, cols].astype(BF16)
            for i in range(0, B, 16):
                y = tv[c, i : i + 16] * x[None]
                y = (y[:, :32] + y[:, 32:]).astype(F32)
                gap = jnp.sum(jnp.sum(y.reshape(16, 4, 8, L), axis=1), axis=1)
                ratio = gap / tl[pl.ds(c, 1), :]
                force[i : i + 16, cols] = (gap / jnp.sqrt(1.0 + ratio * ratio)).astype(BF16)
        low = pl.multiple_of(p * 2 * L, 2 * L)
        pair = pl.ds(low, 2 * L)
        into = pl.ds(low, T + 2 * L)
        slotted[into] = slotted[into] + lax.dot_general(
            hot_d[into, pair], force[:, pair], (((1,), (1,)), ((), ())), preferred_element_type=F32
        )
        return 0

    lax.fori_loop(0, NC // 2, two_columns, 0)
    send[...] = slotted[...].astype(BF16)

    def force_copy(k):
        d = lax.rem(me + k, ND)
        return pltpu.make_async_remote_copy(
            send.at[pl.ds(pl.multiple_of(d * CAP, CAP), CAP)], got.at[pl.ds(pl.multiple_of(k * CAP, CAP), CAP)],
            frc_s, frc_r.at[k // 32], device_id=(d // NT, lax.rem(d, NT)), device_id_type=MESH,
        )

    def start_force(k, _):
        force_copy(k).start()
        return 0

    lax.fori_loop(1, ND, start_force, 0, unroll=True)
    got[:CAP] = send[pl.ds(pl.multiple_of(me * CAP, CAP), CAP)]

    loads[6].wait()
    to_right.wait()
    to_left.wait()
    before = jnp.where(me == 0, 0.0, rim[0].astype(F32)).astype(BF16)
    after = jnp.where(me == ND - 1, 0.0, rim[1].astype(F32)).astype(BF16)
    wide = jnp.concatenate([before, sd[...], after], axis=1)
    for c in range(2):
        loads[8 + NC + c].wait()
        cols = slice(c * L, (c + 1) * L)
        near = wide[:, c * L : c * L + 3 * L]
        for k in range(7):
            at = sc[k : k + 1, cols] + (96 - c * L)
            picked = jnp.dot(near, one_hot(at == iota((3 * L, L), 0)), preferred_element_type=F32)
            acc[k] = picked.astype(BF16)

        def more(i, _, c=c, cols=cols):
            some = pl.ds(pl.multiple_of(i * 8, 8), 8)
            total = jnp.zeros((8, 8, L), F32)
            for k in range(7):
                y = sv[c, k, some] * acc[k][None]
                y = (y[:, :32] + y[:, 32:]).astype(F32)
                total = total + jnp.sum(y.reshape(8, 4, 8, L), axis=1)
            image[some, cols] = jnp.sum(total, axis=1)
            return 0

        lax.fori_loop(0, B // 8, more, 0, unroll=2)

    loads[7].wait()
    total = image[...] - ld[...]
    for j in range(4):
        n = 32 * CAP - (CAP if j == 0 else 0)
        pltpu.make_async_remote_copy(
            send.at[pl.ds(0, n)], got.at[pl.ds(0, n)], frc_s, frc_r.at[j], device_id=(g, t), device_id_type=MESH
        ).wait_recv()
        part = got[j * 32 * CAP : (j + 1) * 32 * CAP]
        spread = one_hot(part[:, B : B + 1].astype(F32).astype(I32) == iota((32 * CAP, 256), 1))
        total = total + lax.dot_general(part, spread, (((0,), (0,)), ((), ())), preferred_element_type=F32)[:B]
    out[...] = total
    n = (ND - 1) * CAP
    pltpu.make_async_remote_copy(
        send.at[pl.ds(0, n)], got.at[pl.ds(0, n)], frc_s, frc_r.at[0], device_id=(g, t), device_id_type=MESH
    ).wait_send()


def on_device(
    soil_disp, soil_vals, soil_cols, load, pile_disp, tie_vals, tie_pile, tie_limit, tie_dest, tie_block
):
    lanes = [x.reshape(NC, L) for x in (tie_pile, tie_limit, tie_dest, tie_block)]
    args = [soil_disp, soil_vals, soil_cols, load, pile_disp, tie_vals, *lanes]
    tiles = {1: (2, 7, B, B, L), 5: (NC, B, B, L)}
    dma = pltpu.SemaphoreType.DMA
    return pl.pallas_call(
        kernel,
        out_shape=jax.ShapeDtypeStruct(load.shape, F32),
        in_specs=[pl.BlockSpec(memory_space=pl.ANY)] * len(args),
        out_specs=pl.BlockSpec(memory_space=pltpu.VMEM),
        scratch_shapes=[
            *[pltpu.VMEM(tiles.get(n, x.shape), x.dtype) for n, x in enumerate(args)],
            pltpu.VMEM((NT, PCAP, T), BF16),
            pltpu.VMEM((ND * CAP, T), BF16),
            pltpu.VMEM((NT, 1, L), I32),
            pltpu.VMEM((NT, 1, L), I32),
            pltpu.VMEM((NT, B, L), BF16),
            pltpu.VMEM((NT, B, L), BF16),
            pltpu.VMEM((B, T), F32),
            pltpu.VMEM((L, T), BF16),
            pltpu.VMEM((ND * CAP, L), F32),
            pltpu.VMEM((ND * CAP, L), BF16),
            pltpu.VMEM((ND * CAP, L), BF16),
            pltpu.VMEM((2, B, L), BF16),
            pltpu.VMEM((7, B, L), BF16),
            pltpu.VMEM((B, 256), F32),
            dma((8 + NC + 2,)),
            dma((NT,)), dma((NT,)), dma((NT,)), dma((NT,)), dma((2,)), dma((2,)), dma, dma((4,)),
            pltpu.SemaphoreType.REGULAR,
        ],
        compiler_params=pltpu.CompilerParams(
            collective_id=0, has_side_effects=True, vmem_limit_bytes=56 * 1024 * 1024
        ),
        cost_estimate=pl.CostEstimate(flops=3_000_000_000, bytes_accessed=24_000_000, transcendentals=65536),
        name="residual",
    )(*args)


def solution(mesh):
    both = ("grp", "tie")
    return jax.shard_map(
        on_device,
        mesh=mesh,
        in_specs=(
            P(None, both), P(None, None, None, both), P(None, both), P(None, both), P(None, both),
            P(None, None, both), P(both), P(both), P(both), P(both),
        ),
        out_specs=P(None, both),
        check_vma=False,
    )
```

```python
import jax
import jax.numpy as jnp
from jax import lax
from jax.experimental import pallas as pl
from jax.experimental.pallas import tpu as pltpu
from jax.sharding import PartitionSpec as P

MESH = pl.DeviceIdType.MESH
F32, BF16, I32 = jnp.float32, jnp.bfloat16, jnp.int32
NT, NG = 16, 8
ND = NT * NG
PCAP, CAP = 128, 16
B = 64
T = 1024
L = 128
NC = T // L


def one_hot(cond):
    return jnp.where(cond, 1.0, 0.0).astype(BF16)


def iota(shape, dim):
    return lax.broadcasted_iota(I32, shape, dim)


def slots(ids, n, cap):
    before = iota((L, 2 * L), 0)
    now = iota((L, 2 * L), 1)
    tri = one_hot((before < now) | (now >= L))
    rows = [ids[c : c + 1, :] == iota((n, L), 0) for c in range(NC)]
    hot = jnp.concatenate([one_hot(r) for r in rows], axis=0)
    sums = jnp.dot(hot, tri, preferred_element_type=F32)
    run = jnp.zeros((n, L), F32)
    out = []
    for c in range(NC):
        part = sums[c * n : (c + 1) * n]
        rank = jnp.sum(jnp.where(rows[c], part[:, :L] + run, 0.0), axis=0, keepdims=True)
        out.append(ids[c : c + 1, :] * cap + rank.astype(I32))
        run = run + part[:, L:]
    return out


def kernel(
    soil_disp, soil_vals, soil_cols, load, pile_disp, tie_vals, tie_pile, tie_limit, tie_dest, tie_block,
    out,
    sd, sv, sc, ld, pd, tv, tp, tl, td, tb,
    hot_p, hot_d, ask, asked, answer, piles, state, force, slotted, send, got, rim, acc, image,
    in_sem, ask_s, ask_r, ans_s, ans_r, rim_s, rim_r, frc_s, frc_r, ready,
):
    g, t = lax.axis_index("grp"), lax.axis_index("tie")
    me = g * NT + t
    bar = pltpu.get_barrier_semaphore()

    def greet_tie(k, _):
        pl.semaphore_signal(bar, inc=1, device_id=(g, lax.rem(t + k, NT)), device_id_type=MESH)
        return 0

    def greet_grp(k, _):
        pl.semaphore_signal(bar, inc=1, device_id=(lax.rem(g + k, NG), t), device_id_type=MESH)
        return 0

    lax.fori_loop(1, NT, greet_tie, 0)
    lax.fori_loop(1, NG, greet_grp, 0)

    pairs = [
        (tie_pile, tp), (pile_disp, pd), (tie_dest, td), (tie_block, tb), (tie_limit, tl), (soil_disp, sd),
        (soil_cols, sc), (load, ld),
    ]
    pairs += [(tie_vals.at[:, :, pl.ds(c * L, L)], tv.at[c]) for c in range(NC)]
    pairs += [(soil_vals.at[:, :, :, pl.ds(c * L, L)], sv.at[c]) for c in range(2)]
    loads = {}
    for n, (src, dst) in enumerate(pairs):
        copy = pltpu.make_async_copy(src, dst, in_sem.at[n])
        copy.start()
        loads[n] = copy

    loads[0].wait()
    ids = tp[...]
    holder = ids // T
    seg = ids - holder * T
    where = slots(holder, NT, PCAP)

    def fill_p(h, _):
        for c in range(NC):
            hot_p[h, :, c * L : (c + 1) * L] = one_hot((where[c] - h * PCAP) == iota((PCAP, L), 0))
        return 0

    lax.fori_loop(0, NT, fill_p, 0)
    hi = seg // 32
    lo = seg - hi * 32
    hi_row = jnp.concatenate([hi[c : c + 1, :] for c in range(NC)], axis=1).astype(F32)
    lo_row = jnp.concatenate([lo[c : c + 1, :] for c in range(NC)], axis=1).astype(F32)
    first = iota((16, T), 0)
    digits = jnp.where(first == 0, hi_row, jnp.where(first == 1, lo_row, 0.0)).astype(BF16)

    def fill_ask(q, _):
        named = lax.dot_general(
            digits, hot_p[pl.ds(q * 4, 4)].reshape(4 * PCAP, T), (((1,), (1,)), ((), ())), preferred_element_type=F32
        )
        number = (named[0:1] * 32.0 + named[1:2]).astype(I32)
        for h in range(4):
            ask[q * 4 + h] = number[:, h * L : (h + 1) * L]
        return 0

    lax.fori_loop(0, NT // 4, fill_ask, 0)

    pl.semaphore_wait(bar, NT - 1 + NG - 1)

    def ask_copy(k):
        h = lax.rem(t + k, NT)
        return pltpu.make_async_remote_copy(
            ask.at[h], asked.at[t], ask_s.at[k], ask_r.at[k], device_id=(g, h), device_id_type=MESH
        )

    def start_ask(k, _):
        ask_copy(k).start()
        return 0

    lax.fori_loop(1, NT, start_ask, 0)
    asked[t] = ask[t]

    def greet_again(k, _):
        pl.semaphore_signal(ready, inc=1, device_id=(lax.rem(g + k, NG), t), device_id_type=MESH)
        return 0

    lax.fori_loop(1, NG, greet_again, 0)

    loads[2].wait()
    goes = slots(td[...], ND, CAP)

    def fill_d(m, _):
        for c in range(NC):
            hot_d[pl.ds(m * L, L), c * L : (c + 1) * L] = one_hot((goes[c] - m * L) == iota((L, L), 0))
        return 0

    lax.fori_loop(0, ND * CAP // L, fill_d, 0)

    loads[1].wait()

    def answer_copy(k):
        r = lax.rem(t + k, NT)
        return pltpu.make_async_remote_copy(
            answer.at[r], piles.at[t], ans_s.at[k], ans_r.at[k], device_id=(g, r), device_id_type=MESH
        )

    for q in range(NT // 4):
        hots = []
        for n in range(4):
            if q * 4 + n + 1 < NT:
                ask_copy(NT - (q * 4 + n + 1)).wait()
            r = lax.rem(t + q * 4 + n + 1, NT)
            hots.append(one_hot(asked[r] == iota((T, L), 0)))
        found = jnp.dot(pd[...], jnp.concatenate(hots, axis=1), preferred_element_type=F32).astype(BF16)
        for n in range(4):
            k = q * 4 + n + 1
            block = found[:, n * L : (n + 1) * L]
            if k < NT:
                answer[lax.rem(t + k, NT)] = block
                answer_copy(k).start()
            else:
                piles[t] = block

    pl.semaphore_wait(ready, NG - 1)
    loads[5].wait()
    right, left = lax.rem(me + 1, ND), lax.rem(me + ND - 1, ND)
    to_right = pltpu.make_async_remote_copy(
        sd.at[:, pl.ds(L, L)], rim.at[0], rim_s.at[0], rim_r.at[0],
        device_id=(right // NT, lax.rem(right, NT)), device_id_type=MESH,
    )
    to_left = pltpu.make_async_remote_copy(
        sd.at[:, pl.ds(0, L)], rim.at[1], rim_s.at[1], rim_r.at[1],
        device_id=(left // NT, lax.rem(left, NT)), device_id_type=MESH,
    )
    to_right.start()
    to_left.start()

    for q in range(NT // 4):
        for n in range(4):
            if q * 4 + n > 0:
                answer_copy(q * 4 + n).wait()
        held = [lax.rem(t + NT - (q * 4 + n), NT) for n in range(4)]
        left_side = jnp.concatenate([piles[h] for h in held], axis=1)
        right_side = jnp.concatenate([hot_p[h] for h in held], axis=0)
        part = jnp.dot(left_side, right_side, preferred_element_type=F32)
        state[...] = part if q == 0 else state[...] + part

    loads[3].wait()
    loads[4].wait()
    slotted[...] = jnp.zeros_like(slotted)
    force[B:] = jnp.zeros((B, T), BF16)
    for c in range(NC):
        force[B : B + 16, c * L : (c + 1) * L] = jnp.where(
            iota((16, L), 0) == 0, tb[c : c + 1, :].astype(F32), 0.0
        ).astype(BF16)
        loads[8 + c].wait()

    def two_columns(p, _):
        for n in range(2):
            c = p * 2 + n
            cols = pl.ds(pl.multiple_of(c * L, L), L)
            x = state[:, cols].astype(BF16)
            for i in range(0, B, 16):
                y = tv[c, i : i + 16] * x[None]
                y = (y[:, :32] + y[:, 32:]).astype(F32)
                gap = jnp.sum(jnp.sum(y.reshape(16, 4, 8, L), axis=1), axis=1)
                ratio = gap / tl[pl.ds(c, 1), :]
                force[i : i + 16, cols] = (gap / jnp.sqrt(1.0 + ratio * ratio)).astype(BF16)
        low = pl.multiple_of(p * 2 * L, 2 * L)
        pair = pl.ds(low, 2 * L)
        into = pl.ds(low, T + 2 * L)
        slotted[into] = slotted[into] + lax.dot_general(
            hot_d[into, pair], force[:, pair], (((1,), (1,)), ((), ())), preferred_element_type=F32
        )
        return 0

    lax.fori_loop(0, NC // 2, two_columns, 0)
    send[...] = slotted[...].astype(BF16)

    def force_copy(k):
        d = lax.rem(me + k, ND)
        return pltpu.make_async_remote_copy(
            send.at[pl.ds(pl.multiple_of(d * CAP, CAP), CAP)], got.at[pl.ds(pl.multiple_of(k * CAP, CAP), CAP)],
            frc_s, frc_r.at[k // 32], device_id=(d // NT, lax.rem(d, NT)), device_id_type=MESH,
        )

    def start_force(k, _):
        force_copy(k).start()
        return 0

    lax.fori_loop(1, ND, start_force, 0, unroll=True)
    got[:CAP] = send[pl.ds(pl.multiple_of(me * CAP, CAP), CAP)]

    loads[6].wait()
    to_right.wait()
    to_left.wait()
    before = jnp.where(me == 0, 0.0, rim[0].astype(F32)).astype(BF16)
    after = jnp.where(me == ND - 1, 0.0, rim[1].astype(F32)).astype(BF16)
    wide = jnp.concatenate([before, sd[...], after], axis=1)
    for c in range(2):
        loads[8 + NC + c].wait()
        cols = slice(c * L, (c + 1) * L)
        near = wide[:, c * L : c * L + 3 * L]
        for k in range(7):
            at = sc[k : k + 1, cols] + (96 - c * L)
            picked = jnp.dot(near, one_hot(at == iota((3 * L, L), 0)), preferred_element_type=F32)
            acc[k] = picked.astype(BF16)

        def more(i, _, c=c, cols=cols):
            some = pl.ds(pl.multiple_of(i * 8, 8), 8)
            total = jnp.zeros((8, 8, L), F32)
            for k in range(7):
                y = sv[c, k, some].astype(F32) * acc[k].astype(F32)[None]
                total = total + jnp.sum(y.reshape(8, 8, 8, L), axis=1)
            image[some, cols] = jnp.sum(total, axis=1)
            return 0

        lax.fori_loop(0, B // 8, more, 0, unroll=2)

    loads[7].wait()
    total = image[...] - ld[...]
    for j in range(4):
        n = 32 * CAP - (CAP if j == 0 else 0)
        pltpu.make_async_remote_copy(
            send.at[pl.ds(0, n)], got.at[pl.ds(0, n)], frc_s, frc_r.at[j], device_id=(g, t), device_id_type=MESH
        ).wait_recv()
        part = got[j * 32 * CAP : (j + 1) * 32 * CAP]
        spread = one_hot(part[:, B : B + 1].astype(F32).astype(I32) == iota((32 * CAP, 256), 1))
        total = total + lax.dot_general(part, spread, (((0,), (0,)), ((), ())), preferred_element_type=F32)[:B]
    out[...] = total
    n = (ND - 1) * CAP
    pltpu.make_async_remote_copy(
        send.at[pl.ds(0, n)], got.at[pl.ds(0, n)], frc_s, frc_r.at[0], device_id=(g, t), device_id_type=MESH
    ).wait_send()


def on_device(
    soil_disp, soil_vals, soil_cols, load, pile_disp, tie_vals, tie_pile, tie_limit, tie_dest, tie_block
):
    lanes = [x.reshape(NC, L) for x in (tie_pile, tie_limit, tie_dest, tie_block)]
    args = [soil_disp, soil_vals, soil_cols, load, pile_disp, tie_vals, *lanes]
    tiles = {1: (2, 7, B, B, L), 5: (NC, B, B, L)}
    dma = pltpu.SemaphoreType.DMA
    return pl.pallas_call(
        kernel,
        out_shape=jax.ShapeDtypeStruct(load.shape, F32),
        in_specs=[pl.BlockSpec(memory_space=pl.ANY)] * len(args),
        out_specs=pl.BlockSpec(memory_space=pltpu.VMEM),
        scratch_shapes=[
            *[pltpu.VMEM(tiles.get(n, x.shape), x.dtype) for n, x in enumerate(args)],
            pltpu.VMEM((NT, PCAP, T), BF16),
            pltpu.VMEM((ND * CAP, T), BF16),
            pltpu.VMEM((NT, 1, L), I32),
            pltpu.VMEM((NT, 1, L), I32),
            pltpu.VMEM((NT, B, L), BF16),
            pltpu.VMEM((NT, B, L), BF16),
            pltpu.VMEM((B, T), F32),
            pltpu.VMEM((L, T), BF16),
            pltpu.VMEM((ND * CAP, L), F32),
            pltpu.VMEM((ND * CAP, L), BF16),
            pltpu.VMEM((ND * CAP, L), BF16),
            pltpu.VMEM((2, B, L), BF16),
            pltpu.VMEM((7, B, L), BF16),
            pltpu.VMEM((B, 256), F32),
            dma((8 + NC + 2,)),
            dma((NT,)), dma((NT,)), dma((NT,)), dma((NT,)), dma((2,)), dma((2,)), dma, dma((4,)),
            pltpu.SemaphoreType.REGULAR,
        ],
        compiler_params=pltpu.CompilerParams(
            collective_id=0, has_side_effects=True, vmem_limit_bytes=56 * 1024 * 1024
        ),
        cost_estimate=pl.CostEstimate(flops=3_000_000_000, bytes_accessed=24_000_000, transcendentals=65536),
        name="residual",
    )(*args)


def solution(mesh):
    both = ("grp", "tie")
    return jax.shard_map(
        on_device,
        mesh=mesh,
        in_specs=(
            P(None, both), P(None, None, None, both), P(None, both), P(None, both), P(None, both),
            P(None, None, both), P(both), P(both), P(both), P(both),
        ),
        out_specs=P(None, both),
        check_vma=False,
    )
```
